512 devices in a mesh: replica: 32 (over z, y_lo), fsdp: 16 (over x, y_hi, core).
Axes of the slice: x: 4, y: 4 (y_hi: 2, y_lo: 2; y = y_hi * 2 + y_lo), z: 16, core: 2. Of those that a mesh axis runs over, the one named last changes fastest.
Arguments:
- tokens: bfloat16 [32, 2048, 4096], P('replica', 'fsdp'), may hold values from -6 to 6
- local_weight: bfloat16 [32, 4096, 512], P('replica', 'fsdp'), may hold values from -6 to 6
- key_cot: bfloat16 [32, 2048, 512], P('replica', 'fsdp'), may hold values from -6 to 6
- global_weight: float32 [4096, 512], P(('fsdp', 'replica')), may hold values from -6 to 6
- momentum: float32 [4096, 512], P(('fsdp', 'replica')), may hold values from -6 to 6
- anchor: float32 [4096, 512], P(('fsdp', 'replica')), may hold values from -6 to 6
Outputs:
- keys: bfloat16 [32, 2048, 512], P('replica', 'fsdp')
- grad_tokens: bfloat16 [32, 2048, 4096], P('replica', 'fsdp')
- grad_weight: bfloat16 [32, 4096, 512], P('replica', 'fsdp')
- momentum_new: float32 [4096, 512], P(('fsdp', 'replica'))
- global_new: float32 [4096, 512], P(('fsdp', 'replica'))
- synced: bfloat16 [4096, 512], P('fsdp')
The draws below stay inside these ranges and needn't reach their ends.
All inputs are finite; a program needn't handle non-finite values.
Results may differ from the reference program's by a relative error of at most 0.0095.
Values may be sent and summed in bfloat16 or wider, within the bound.
A program may use at most 64 MiB of HBM per device.

```python
import jax
import jax.numpy as jnp
from jax import lax

D_WIN = 4096
KVW = 512
TOK_R = 2048
N_REPLICA = 32


def strengthened(values, stream_key, source, target, shards_of, factor):
    owner, partner = [(jnp.arange(values.shape[dim]) // (values.shape[dim] // shards_of)).reshape([-1 if axis == dim else 1 for axis in range(values.ndim)]) for dim in (source, target)]
    chosen = jax.random.permutation(stream_key, shards_of)[partner]
    strong = (owner == chosen) | (owner == (partner + shards_of // 2) % shards_of)
    return jnp.where(strong, factor * values, values)


def block_levels(key, extent, cuts, least, largest):
    factor_of = 1.0
    for axis_at, parts in cuts:
        heights = jax.random.uniform(jax.random.fold_in(jax.random.fold_in(key, 6), axis_at), (parts,), jnp.float32, least / len(cuts), largest / len(cuts))
        factor_of = factor_of * jnp.repeat(jnp.exp(heights), extent[axis_at] // parts).reshape((-1,) + (1,) * (len(extent) - 1 - axis_at))
    return factor_of


def scatter_about(stream_key, shape, width, bound, shards=(), held_as=jnp.bfloat16):
    array = width * jax.random.normal(stream_key, shape, jnp.float32)
    if shards:
        array = array * block_levels(stream_key, shape, shards, -0.22, 0.18)
    return jnp.clip(array, -bound, bound).astype(held_as)


def bell_draw_with(stream_key, dims, scale, most, shards, heavy, held_as=jnp.bfloat16):
    values = scale * jax.random.normal(stream_key, dims, jnp.float32)
    if shards:
        values = values * block_levels(stream_key, dims, shards, -0.22, 0.18)
    return jnp.clip(strengthened(values, jax.random.fold_in(stream_key, 3), *heavy), -most, most).astype(held_as)


def setup_inputs(seed: int = 0) -> dict:
    arg_keys = jax.random.split(jax.random.key(seed), 7)
    tokens = scatter_about(arg_keys[0], (N_REPLICA, TOK_R, D_WIN), 1.0, 6.0, ((0, 32), (1, 16)))
    local_weight = bell_draw_with(arg_keys[1], (N_REPLICA, D_WIN, KVW), 1.0, 6.0, ((0, 32), (1, 16)), (0, 1, 32, 2.75))
    key_cot = scatter_about(arg_keys[2], (N_REPLICA, TOK_R, KVW), 1.0, 6.0, ((0, 32), (1, 16)))
    global_weight = scatter_about(arg_keys[3], (D_WIN, KVW), 1.0, 6.0, ((0, 512),), jnp.float32)
    momentum = scatter_about(arg_keys[4], (D_WIN, KVW), 1.0, 6.0, ((0, 512),), jnp.float32)
    anchor = scatter_about(arg_keys[5], (D_WIN, KVW), 1.0, 6.0, ((0, 512),), jnp.float32)
    return dict(tokens=tokens, local_weight=local_weight, key_cot=key_cot, global_weight=global_weight, momentum=momentum, anchor=anchor)


def reference(tokens, local_weight, key_cot, global_weight, momentum, anchor):
    scale = 1.0 / (D_WIN ** 0.5)

    def worker(items):
        inputs, weight, cot = items
        made = (jnp.dot(inputs, weight, preferred_element_type=jnp.float32) * scale).astype(jnp.bfloat16)
        back = (jnp.dot(cot, weight.T, preferred_element_type=jnp.float32) * scale).astype(jnp.bfloat16)
        wgrad = (jnp.dot(inputs.T, cot, preferred_element_type=jnp.float32) * scale).astype(jnp.bfloat16)
        return made, back, wgrad

    keys, grad_tokens, grad_weight = lax.map(worker, (tokens, local_weight, key_cot))
    total = jnp.sum(local_weight.astype(jnp.float32), axis=0)
    pseudo = global_weight - total / N_REPLICA
    push = pseudo + 0.1 * (global_weight - anchor)
    momentum_new = 0.9 * momentum + push
    global_new = global_weight - 0.7 * (push + 0.9 * momentum_new)
    synced = global_new.astype(jnp.bfloat16)
    return keys, grad_tokens, grad_weight, momentum_new, global_new, synced
```

```python
import jax
import jax.numpy as jnp
from jax import lax
from jax.experimental import pallas as pl
from jax.experimental.pallas import tpu as pltpu
from jax.sharding import PartitionSpec as P

MESH = pl.DeviceIdType.MESH
BF16, F32 = jnp.bfloat16, jnp.float32
SCALE = 1.0 / 4096**0.5
N_REPLICA = 32
NX, NZ = 4, 16
TOK, ROWS, KVW = 128, 256, 512


def kernel(
    tok, w, cot, glob, mom, anc,
    keys_o, gt_o, dw_o, mom_o, glob_o, syn_o,
    wbuf, tokv, tbuf, cbuf, acc, dwacc, gsend, grecv, sbuf, ybuf, zsum, rbuf, gma, res,
    ss_w, rs_w, ss_t, rs_t, ss_c, rs_c, ss_g, rs_g, ss_y, rs_y, ss_z, rs_z,
    ss_b, rs_b, ss_f, rs_f, ss_p, rs_p, ss_q, rs_q, loc,
):
    r, f = lax.axis_index("replica"), lax.axis_index("fsdp")
    z, yl = r // 2, r % 2
    x, yh, c = f // 4, (f // 2) % 2, f % 2
    xp, xm, x2 = (x + 1) % NX, (x + 3) % NX, (x + 2) % NX
    odd = (z + yl) % 2

    def at_x(other):
        return (r, other * 4 + yh * 2 + c)

    core = (r, x * 4 + yh * 2 + (1 - c))
    side = (r, x * 4 + (1 - yh) * 2 + c)
    cross = (r, x * 4 + (1 - yh) * 2 + (1 - c))
    pair = (z * 2 + (1 - yl), f)
    right, left, far = at_x(xp), at_x(xm), at_x(x2)

    def at_z(step):
        return (((z + step) % NZ) * 2 + yl, f)

    def remote(src, dst, send_sem, recv_sem, device):
        return pltpu.make_async_remote_copy(
            src_ref=src, dst_ref=dst, send_sem=send_sem, recv_sem=recv_sem,
            device_id=device, device_id_type=MESH,
        )

    def columns(xx, hh, cc):
        return pl.ds(pl.multiple_of((xx * 4 + hh * 2 + cc) * ROWS, ROWS), ROWS)

    xs_t = (x, xp, xm, x2)
    local = [
        pltpu.make_async_copy(w, wbuf.at[0], loc.at[0]),
        pltpu.make_async_copy(tok, tokv, loc.at[1]),
        pltpu.make_async_copy(cot, cbuf.at[pl.ds(0, TOK)], loc.at[2]),
        pltpu.make_async_copy(w.at[:, yl], sbuf, loc.at[3]),
        pltpu.make_async_copy(glob, gma.at[yl, 0], loc.at[4]),
        pltpu.make_async_copy(mom, gma.at[yl, 1], loc.at[5]),
        pltpu.make_async_copy(anc, gma.at[yl, 2], loc.at[6]),
    ] + [
        pltpu.make_async_copy(
            tok.at[:, columns(xs_t[i], yh, c)], tbuf.at[i, pl.ds(0, TOK)], loc.at[7 + i]
        )
        for i in range(4)
    ]
    for copy in local:
        copy.start()

    barrier = pltpu.get_barrier_semaphore()
    peers = [right, left, far, core, side, cross, pair] + [at_z(d) for d in range(1, NZ)]
    for peer in peers:
        pl.semaphore_signal(barrier, inc=1, device_id=peer, device_id_type=MESH)
    pl.semaphore_wait(barrier, len(peers))

    def half(ref, h):
        return ref.at[pl.ds(4 * h, 4)]

    sent = []

    def go(copy):
        copy.start()
        sent.append(copy)

    def w_send(src, slot, h, device):
        k = 2 * slot + h
        go(remote(src, half(wbuf.at[slot], h), ss_w.at[k], rs_w.at[k], device))

    def w_wait(slot, h):
        k = 2 * slot + h
        there = half(wbuf.at[slot], h)
        remote(there, there, ss_w.at[k], rs_w.at[k], core).wait_recv()

    def w_fwd(slot, h, to, device):
        w_send(half(wbuf.at[slot], h), to, h, device)

    go(remote(w.at[:, 1 - yl], ybuf, ss_y.at[0], rs_y.at[0], pair))
    w_send(half(w, 0), 1, 0, right)
    w_send(half(w, 1), 2, 1, left)
    w_send(half(w, 0), 4, 0, side)
    w_send(half(w, 0), 8, 0, core)
    w_send(half(w, 1), 8, 1, core)
    w_send(half(w, 1), 1, 1, right)
    w_send(half(w, 0), 2, 0, left)
    w_send(half(w, 1), 4, 1, side)

    def c_send(src, s, device):
        go(remote(src, cbuf.at[pl.ds(s * TOK, TOK)], ss_c.at[s], rs_c.at[s], device))

    def c_wait(s):
        there = cbuf.at[pl.ds(s * TOK, TOK)]
        remote(there, there, ss_c.at[s], rs_c.at[s], core).wait_recv()

    c_send(cot, 2, side)
    c_send(cot, 1, core)

    def t_send(i, s, hh, cc, device):
        k = 4 * i + s
        go(remote(
            tok.at[:, columns(xs_t[i], hh, cc)], tbuf.at[i, pl.ds(s * TOK, TOK)],
            ss_t.at[k], rs_t.at[k], device,
        ))

    def t_wait(i, s):
        there = tbuf.at[i, pl.ds(s * TOK, TOK)]
        remote(there, there, ss_t.at[4 * i + s], rs_t.at[4 * i + s], core).wait_recv()

    for i in (1, 2, 3, 0):
        t_send(i, 2, 1 - yh, c, side)
        t_send(i, 3, 1 - yh, 1 - c, cross)
        t_send(i, 1, yh, 1 - c, core)

    def p_copies():
        return [
            remote(src, gma.at[yl, n], ss_p.at[n], rs_p.at[n], pair)
            for n, src in enumerate((glob, mom, anc))
        ]

    @pl.when(odd == 1)
    def _():
        for copy in p_copies():
            copy.start()

    xs_w = (x, xm, xp, x2)

    def block(slot, first=False):
        cols = columns(
            xs_w[slot % 4],
            yh if slot % 8 < 4 else 1 - yh,
            c if slot < 8 else 1 - c,
        )
        weight = wbuf[slot].reshape(ROWS, KVW)
        part = jnp.dot(tokv[:, cols], weight, preferred_element_type=F32)
        if first:
            acc[...] = part
        else:
            acc[...] += part
        back = lax.dot_general(
            cbuf[0:TOK], weight, (((1,), (1,)), ((), ())), preferred_element_type=F32
        )
        gt_o[:, cols] = (back * SCALE).astype(BF16)

    def partial_sum(i):
        return lax.dot_general(
            tbuf[i], cbuf[...], (((0,), (0,)), ((), ())), preferred_element_type=F32
        )

    def g_copy(i):
        device = (None, right, left, far)[i]
        return remote(
            gsend.at[i - 1], grecv.at[i - 1], ss_g.at[i - 1], rs_g.at[i - 1], device
        )

    local[0].wait()
    local[1].wait()
    local[2].wait()
    block(0, first=True)
    w_wait(8, 0)
    w_wait(8, 1)
    block(8)

    local[3].wait()
    remote(ybuf, ybuf, ss_y.at[0], rs_y.at[0], pair).wait_recv()
    zsum[...] = (sbuf[...].astype(F32) + ybuf[...].astype(F32)).astype(BF16)

    def z_copy(j):
        step = 2 * j + odd
        return remote(
            zsum.at[((z + step) % NZ) // 2], rbuf.at[step], ss_z.at[j], rs_z.at[step], at_z(step)
        )

    for j in (4, 3, 5, 2, 6, 1, 7):
        z_copy(j).start()

    @pl.when(odd == 1)
    def _():
        z_copy(0).start()

    w_wait(1, 0)
    w_fwd(1, 0, 3, right)
    w_wait(2, 1)
    w_fwd(2, 1, 3, left)
    w_wait(4, 0)
    w_fwd(4, 0, 5, right)
    w_fwd(1, 0, 9, core)
    w_fwd(2, 1, 10, core)
    w_fwd(4, 0, 12, core)
    w_wait(4, 1)
    w_fwd(4, 1, 6, left)
    w_fwd(4, 1, 5, right)
    w_fwd(4, 0, 6, left)
    w_fwd(4, 1, 12, core)
    w_wait(1, 1)
    w_fwd(1, 1, 9, core)
    w_wait(2, 0)
    w_fwd(2, 0, 10, core)
    block(1)
    block(2)
    block(4)
    for slot in (9, 10, 12):
        w_wait(slot, 0)
        w_wait(slot, 1)
        block(slot)
    c_wait(2)
    c_send(cbuf.at[pl.ds(2 * TOK, TOK)], 3, core)
    w_wait(3, 0)
    w_fwd(3, 0, 11, core)
    w_wait(3, 1)
    w_fwd(3, 1, 11, core)
    block(3)
    w_wait(11, 0)
    w_wait(11, 1)
    block(11)

    def make_partial(i):
        local[7 + i].wait()
        for s in (1, 2, 3):
            t_wait(i, s)
        if i == 0:
            dwacc[...] = partial_sum(0)
        else:
            gsend[i - 1] = partial_sum(i).astype(BF16)
            go(g_copy(i))

    c_wait(1)
    c_wait(3)
    make_partial(1)

    for n in (4, 5, 6):
        local[n].wait()

    def syn_copy(d):
        return remote(syn_o.at[z], syn_o.at[z], ss_b.at[d], rs_b.at[d], at_z(d))

    def res_copies():
        return [
            remote(res.at[1 - yl, n], res.at[1 - yl, n], ss_q.at[n], rs_q.at[n], pair)
            for n in range(2)
        ]

    @pl.when(odd == 0)
    def _():
        rbuf[0] = zsum[z // 2]
        for copy in p_copies():
            copy.wait_recv()
        for d in range(1, NZ):
            remote(rbuf.at[d], rbuf.at[d], ss_z.at[0], rs_z.at[d], pair).wait_recv()
        total = rbuf[0].astype(F32)
        for d in range(1, NZ):
            total = total + rbuf[d].astype(F32)
        fresh = []
        for owner in range(2):
            g, m, a = gma[owner, 0], gma[owner, 1], gma[owner, 2]
            pseudo = g - total[8 * owner : 8 * owner + 8] / N_REPLICA
            push = pseudo + 0.1 * (g - a)
            m_new = 0.9 * m + push
            g_new = g - 0.7 * (push + 0.9 * m_new)
            res[owner, 0] = m_new
            res[owner, 1] = g_new
            fresh.append(g_new)
        syn_o[z] = jnp.concatenate(fresh, axis=0).astype(BF16)
        for d in (8, 7, 9, 6, 10, 5, 11, 4, 12, 3, 13, 2, 14, 1, 15):
            syn_copy(d).start()
        for copy in res_copies():
            copy.start()

    w_wait(5, 0)
    w_fwd(5, 0, 7, right)
    w_wait(6, 1)
    w_fwd(6, 1, 7, left)
    w_fwd(5, 0, 13, core)
    w_fwd(6, 1, 14, core)
    make_partial(2)
    w_wait(5, 1)
    w_fwd(5, 1, 13, core)
    w_wait(6, 0)
    w_fwd(6, 0, 14, core)
    block(5)
    block(6)
    make_partial(3)
    for slot in (13, 14):
        w_wait(slot, 0)
        w_wait(slot, 1)
        block(slot)
    w_wait(7, 0)
    w_fwd(7, 0, 15, core)
    w_wait(7, 1)
    w_fwd(7, 1, 15, core)
    block(7)
    make_partial(0)
    w_wait(15, 0)
    w_wait(15, 1)
    block(15)
    keys_o[...] = (acc[...] * SCALE).astype(BF16)

    def hand(j):
        place = (z - 2 * j - odd + NZ) % NZ
        return remote(syn_o.at[place], syn_o.at[place], ss_f.at[j], rs_f.at[j], pair)

    def taken(j):
        place = (z - 2 * j - (1 - odd) + NZ) % NZ
        return remote(syn_o.at[place], syn_o.at[place], ss_f.at[j], rs_f.at[j], pair)

    def arrive(j):
        step = 2 * j + odd
        place = (z - step + NZ) % NZ
        remote(syn_o.at[place], syn_o.at[place], ss_b.at[0], rs_b.at[step], pair).wait_recv()

    @pl.when(odd == 1)
    def _():
        arrive(0)

    hand(0).start()
    for j in (1, 7, 2, 6, 3, 5, 4):
        arrive(j)
        hand(j).start()

    for i in (1, 2, 3):
        g_copy(i).wait_recv()
    total = dwacc[...]
    for n in range(3):
        total = total + grecv[n].astype(F32)
    dw_o[...] = (total * SCALE).astype(BF16)

    @pl.when(odd == 1)
    def _():
        for n in range(2):
            remote(res.at[yl, n], res.at[yl, n], ss_q.at[n], rs_q.at[n], pair).wait_recv()

    mom_o[...] = res[yl, 0]
    glob_o[...] = res[yl, 1]
    for j in range(8):
        taken(j).wait_recv()

    for copy in sent:
        copy.wait_send()
    for j in range(1, 8):
        z_copy(j).wait_send()
    for j in range(8):
        hand(j).wait_send()

    @pl.when(odd == 1)
    def _():
        z_copy(0).wait_send()
        for copy in p_copies():
            copy.wait_send()

    @pl.when(odd == 0)
    def _():
        for d in range(1, NZ):
            syn_copy(d).wait_send()
        for copy in res_copies():
            copy.wait_send()


def on_device(tokens, local_weight, key_cot, global_weight, momentum, anchor):
    dma, vmem = pltpu.SemaphoreType.DMA, pltpu.VMEM
    scratch = [
        vmem((16, 8, 2, 16, KVW), BF16),
        vmem((TOK, 4096), BF16),
        vmem((4, 4 * TOK, ROWS), BF16),
        vmem((4 * TOK, KVW), BF16),
        vmem((TOK, KVW), F32),
        vmem((ROWS, KVW), F32),
        vmem((3, ROWS, KVW), BF16),
        vmem((3, ROWS, KVW), BF16),
        vmem((8, 16, KVW), BF16),
        vmem((8, 16, KVW), BF16),
        vmem((8, 16, KVW), BF16),
        vmem((16, 16, KVW), BF16),
        vmem((2, 3, 8, KVW), F32),
        vmem((2, 2, 8, KVW), F32),
        dma((32,)), dma((32,)),
        dma((16,)), dma((16,)),
        dma((4,)), dma((4,)),
        dma((3,)), dma((3,)),
        dma((1,)), dma((1,)),
        dma((8,)), dma((16,)),
        dma((16,)), dma((16,)),
        dma((8,)), dma((8,)),
        dma((3,)), dma((3,)),
        dma((2,)), dma((2,)),
        dma((11,)),
    ]
    hbm, in_vmem = pl.BlockSpec(memory_space=pl.ANY), pl.BlockSpec(memory_space=vmem)
    keys, gt, dw, mom, glob, syn = pl.pallas_call(
        kernel,
        out_shape=(
            jax.ShapeDtypeStruct((TOK, KVW), BF16),
            jax.ShapeDtypeStruct((TOK, 4096), BF16),
            jax.ShapeDtypeStruct((ROWS, KVW), BF16),
            jax.ShapeDtypeStruct((8, KVW), F32),
            jax.ShapeDtypeStruct((8, KVW), F32),
            jax.ShapeDtypeStruct((16, 16, KVW), BF16),
        ),
        in_specs=[hbm] * 6,
        out_specs=[in_vmem] * 6,
        scratch_shapes=scratch,
        compiler_params=pltpu.CompilerParams(
            collective_id=0, has_side_effects=True, vmem_limit_bytes=40 * 2**20
        ),
        cost_estimate=pl.CostEstimate(
            flops=6 * 128 * 4096 * 512, bytes_accessed=4 * 2**20, transcendentals=0
        ),
        name="step",
    )(
        tokens[0],
        local_weight.reshape(8, 2, 16, KVW),
        key_cot[0],
        global_weight,
        momentum,
        anchor,
    )
    return keys[None], gt[None], dw[None], mom, glob, syn.reshape(ROWS, KVW)


def solution(mesh):
    in_specs = (
        P("replica", "fsdp", None),
        P("replica", "fsdp", None),
        P("replica", "fsdp", None),
        P(("fsdp", "replica"), None),
        P(("fsdp", "replica"), None),
        P(("fsdp", "replica"), None),
    )
    out_specs = (
        P("replica", "fsdp", None),
        P("replica", "fsdp", None),
        P("replica", "fsdp", None),
        P(("fsdp", "replica"), None),
        P(("fsdp", "replica"), None),
        P("fsdp", None),
    )
    return jax.shard_map(
        on_device, mesh=mesh, in_specs=in_specs, out_specs=out_specs, check_vma=False
    )
```

```python
import jax
import jax.numpy as jnp
from jax import lax
from jax.experimental import pallas as pl
from jax.experimental.pallas import tpu as pltpu
from jax.sharding import PartitionSpec as P

MESH = pl.DeviceIdType.MESH
BF16, F32 = jnp.bfloat16, jnp.float32
SCALE = 1.0 / 4096**0.5
N_REPLICA = 32
NX, NZ = 4, 16
TOK, ROWS, KVW = 128, 256, 512


def kernel(
    tok, w, cot, glob, mom, anc,
    keys_o, gt_o, dw_o, mom_o, glob_o, syn_o,
    wbuf, tokv, tbuf, cbuf, acc, dwacc, gsend, grecv, sbuf, ybuf, zsum, rbuf, gma, res,
    ss_w, rs_w, ss_t, rs_t, ss_c, rs_c, ss_g, rs_g, ss_y, rs_y, ss_z, rs_z,
    ss_b, rs_b, ss_f, rs_f, ss_p, rs_p, ss_q, rs_q, loc, here,
):
    r, f = lax.axis_index("replica"), lax.axis_index("fsdp")
    z, yl = r // 2, r % 2
    x, yh, c = f // 4, (f // 2) % 2, f % 2
    xp, xm, x2 = (x + 1) % NX, (x + 3) % NX, (x + 2) % NX
    odd = (z + yl) % 2

    def at_x(other):
        return (r, other * 4 + yh * 2 + c)

    core = (r, x * 4 + yh * 2 + (1 - c))
    side = (r, x * 4 + (1 - yh) * 2 + c)
    cross = (r, x * 4 + (1 - yh) * 2 + (1 - c))
    pair = (z * 2 + (1 - yl), f)
    right, left, far = at_x(xp), at_x(xm), at_x(x2)

    def at_z(step):
        return (((z + step) % NZ) * 2 + yl, f)

    def remote(src, dst, send_sem, recv_sem, device):
        return pltpu.make_async_remote_copy(
            src_ref=src, dst_ref=dst, send_sem=send_sem, recv_sem=recv_sem,
            device_id=device, device_id_type=MESH,
        )

    def columns(xx, hh, cc):
        return pl.ds(pl.multiple_of((xx * 4 + hh * 2 + cc) * ROWS, ROWS), ROWS)

    xs_t = (x, xp, xm, x2)
    local = [
        pltpu.make_async_copy(w, wbuf.at[0], loc.at[0]),
        pltpu.make_async_copy(tok, tokv, loc.at[1]),
        pltpu.make_async_copy(cot, cbuf.at[pl.ds(0, TOK)], loc.at[2]),
        pltpu.make_async_copy(w.at[:, yl], sbuf, loc.at[3]),
        pltpu.make_async_copy(glob, gma.at[yl, 0], loc.at[4]),
        pltpu.make_async_copy(mom, gma.at[yl, 1], loc.at[5]),
        pltpu.make_async_copy(anc, gma.at[yl, 2], loc.at[6]),
    ] + [
        pltpu.make_async_copy(
            tok.at[:, columns(xs_t[i], yh, c)], tbuf.at[i, pl.ds(0, TOK)], loc.at[7 + i]
        )
        for i in range(4)
    ]
    for copy in local:
        copy.start()

    barrier = pltpu.get_barrier_semaphore()
    peers = [right, left, far, core, side, cross, pair]
    for peer in peers:
        pl.semaphore_signal(barrier, inc=1, device_id=peer, device_id_type=MESH)
    late = z >= NZ // 2
    for d in range(1, NZ):
        there = (z + d) % NZ

        @pl.when((there > z) | (late & (there >= NZ // 2)))
        def _():
            pl.semaphore_signal(barrier, inc=1, device_id=at_z(d), device_id_type=MESH)

    pl.semaphore_wait(barrier, len(peers) + jnp.where(late, NZ - 1, z))

    def half(ref, h):
        return ref.at[pl.ds(4 * h, 4)]

    sent = []

    def go(copy):
        copy.start()
        sent.append(copy)

    def w_send(src, slot, h, device):
        k = 2 * slot + h
        go(remote(src, half(wbuf.at[slot], h), ss_w.at[k], rs_w.at[k], device))

    def w_wait(slot, h):
        k = 2 * slot + h
        there = half(wbuf.at[slot], h)
        remote(there, there, ss_w.at[k], rs_w.at[k], core).wait_recv()

    def w_fwd(slot, h, to, device):
        w_send(half(wbuf.at[slot], h), to, h, device)

    go(remote(w.at[:, 1 - yl], ybuf, ss_y.at[0], rs_y.at[0], pair))
    w_send(half(w, 0), 1, 0, right)
    w_send(half(w, 1), 2, 1, left)
    w_send(half(w, 0), 4, 0, side)
    w_send(half(w, 0), 8, 0, core)
    w_send(half(w, 1), 8, 1, core)
    w_send(half(w, 1), 1, 1, right)
    w_send(half(w, 0), 2, 0, left)
    w_send(half(w, 1), 4, 1, side)

    def c_send(src, s, device):
        go(remote(src, cbuf.at[pl.ds(s * TOK, TOK)], ss_c.at[s], rs_c.at[s], device))

    def c_wait(s):
        there = cbuf.at[pl.ds(s * TOK, TOK)]
        remote(there, there, ss_c.at[s], rs_c.at[s], core).wait_recv()

    c_send(cot, 2, side)
    c_send(cot, 1, core)

    def t_send(i, s, hh, cc, device):
        k = 4 * i + s
        go(remote(
            tok.at[:, columns(xs_t[i], hh, cc)], tbuf.at[i, pl.ds(s * TOK, TOK)],
            ss_t.at[k], rs_t.at[k], device,
        ))

    def t_wait(i, s):
        there = tbuf.at[i, pl.ds(s * TOK, TOK)]
        remote(there, there, ss_t.at[4 * i + s], rs_t.at[4 * i + s], core).wait_recv()

    for i in (1, 2, 3, 0):
        t_send(i, 2, 1 - yh, c, side)
        t_send(i, 3, 1 - yh, 1 - c, cross)
        t_send(i, 1, yh, 1 - c, core)

    for d in range(1, NZ):
        there = (z + d) % NZ

        @pl.when((there < z) & (there < NZ // 2))
        def _():
            pl.semaphore_signal(here, inc=1, device_id=at_z(d), device_id_type=MESH)

    def p_copies():
        return [
            remote(src, gma.at[yl, n], ss_p.at[n], rs_p.at[n], pair)
            for n, src in enumerate((glob, mom, anc))
        ]

    @pl.when(odd == 1)
    def _():
        for copy in p_copies():
            copy.start()

    xs_w = (x, xm, xp, x2)

    def block(slot, first=False):
        cols = columns(
            xs_w[slot % 4],
            yh if slot % 8 < 4 else 1 - yh,
            c if slot < 8 else 1 - c,
        )
        weight = wbuf[slot].reshape(ROWS, KVW)
        part = jnp.dot(tokv[:, cols], weight, preferred_element_type=F32)
        if first:
            acc[...] = part
        else:
            acc[...] += part
        back = lax.dot_general(
            cbuf[0:TOK], weight, (((1,), (1,)), ((), ())), preferred_element_type=F32
        )
        gt_o[:, cols] = (back * SCALE).astype(BF16)

    def partial_sum(i):
        return lax.dot_general(
            tbuf[i], cbuf[...], (((0,), (0,)), ((), ())), preferred_element_type=F32
        )

    def g_copy(i):
        device = (None, right, left, far)[i]
        return remote(
            gsend.at[i - 1], grecv.at[i - 1], ss_g.at[i - 1], rs_g.at[i - 1], device
        )

    local[0].wait()
    local[1].wait()
    local[2].wait()
    block(0, first=True)
    w_wait(8, 0)
    w_wait(8, 1)
    block(8)

    local[3].wait()
    remote(ybuf, ybuf, ss_y.at[0], rs_y.at[0], pair).wait_recv()
    zsum[...] = (sbuf[...].astype(F32) + ybuf[...].astype(F32)).astype(BF16)

    def z_copy(j):
        step = 2 * j + odd
        return remote(
            zsum.at[((z + step) % NZ) // 2], rbuf.at[step], ss_z.at[j], rs_z.at[step], at_z(step)
        )

    def z_sends():
        for j in (4, 3, 5, 2, 6, 1, 7):
            z_copy(j).start()

        @pl.when(odd == 1)
        def _():
            z_copy(0).start()

    @pl.when(late)
    def _():
        z_sends()

    middle = (z >= NZ // 4) & (z < NZ // 2)
    early = z < NZ // 4

    w_wait(1, 0)
    w_fwd(1, 0, 3, right)
    w_wait(2, 1)
    w_fwd(2, 1, 3, left)
    w_wait(4, 0)
    w_fwd(4, 0, 5, right)
    w_fwd(1, 0, 9, core)
    w_fwd(2, 1, 10, core)
    w_fwd(4, 0, 12, core)
    w_wait(4, 1)
    w_fwd(4, 1, 6, left)
    w_fwd(4, 1, 5, right)
    w_fwd(4, 0, 6, left)
    w_fwd(4, 1, 12, core)
    w_wait(1, 1)
    w_fwd(1, 1, 9, core)
    w_wait(2, 0)
    w_fwd(2, 0, 10, core)
    block(1)
    block(2)
    block(4)
    for slot in (9, 10, 12):
        w_wait(slot, 0)
        w_wait(slot, 1)
        block(slot)

    @pl.when(middle)
    def _():
        pl.semaphore_wait(here, NZ - 1 - z)
        z_sends()

    c_wait(2)
    c_send(cbuf.at[pl.ds(2 * TOK, TOK)], 3, core)
    w_wait(3, 0)
    w_fwd(3, 0, 11, core)
    w_wait(3, 1)
    w_fwd(3, 1, 11, core)
    block(3)
    w_wait(11, 0)
    w_wait(11, 1)
    block(11)

    def make_partial(i):
        local[7 + i].wait()
        for s in (1, 2, 3):
            t_wait(i, s)
        if i == 0:
            dwacc[...] = partial_sum(0)
        else:
            gsend[i - 1] = partial_sum(i).astype(BF16)
            go(g_copy(i))

    c_wait(1)
    c_wait(3)
    make_partial(1)

    @pl.when(early)
    def _():
        pl.semaphore_wait(here, NZ - 1 - z)
        z_sends()

    for n in (4, 5, 6):
        local[n].wait()

    def syn_copy(d):
        return remote(syn_o.at[z], syn_o.at[z], ss_b.at[d], rs_b.at[d], at_z(d))

    def res_copies():
        return [
            remote(res.at[1 - yl, n], res.at[1 - yl, n], ss_q.at[n], rs_q.at[n], pair)
            for n in range(2)
        ]

    def update():
        rbuf[0] = zsum[z // 2]
        for copy in p_copies():
            copy.wait_recv()
        for d in range(1, NZ):
            remote(rbuf.at[d], rbuf.at[d], ss_z.at[0], rs_z.at[d], pair).wait_recv()
        total = rbuf[0].astype(F32)
        for d in range(1, NZ):
            total = total + rbuf[d].astype(F32)
        fresh = []
        for owner in range(2):
            g, m, a = gma[owner, 0], gma[owner, 1], gma[owner, 2]
            pseudo = g - total[8 * owner : 8 * owner + 8] / N_REPLICA
            push = pseudo + 0.1 * (g - a)
            m_new = 0.9 * m + push
            g_new = g - 0.7 * (push + 0.9 * m_new)
            res[owner, 0] = m_new
            res[owner, 1] = g_new
            fresh.append(g_new)
        syn_o[z] = jnp.concatenate(fresh, axis=0).astype(BF16)
        for d in (8, 7, 9, 6, 10, 5, 11, 4, 12, 3, 13, 2, 14, 1, 15):
            syn_copy(d).start()
        for copy in res_copies():
            copy.start()

    @pl.when((odd == 0) & late)
    def _():
        update()

    w_wait(5, 0)
    w_fwd(5, 0, 7, right)
    w_wait(6, 1)
    w_fwd(6, 1, 7, left)
    w_fwd(5, 0, 13, core)
    w_fwd(6, 1, 14, core)
    make_partial(2)
    w_wait(5, 1)
    w_fwd(5, 1, 13, core)
    w_wait(6, 0)
    w_fwd(6, 0, 14, core)
    block(5)
    block(6)
    make_partial(3)

    @pl.when((odd == 0) & middle)
    def _():
        update()

    for slot in (13, 14):
        w_wait(slot, 0)
        w_wait(slot, 1)
        block(slot)
    w_wait(7, 0)
    w_fwd(7, 0, 15, core)
    w_wait(7, 1)
    w_fwd(7, 1, 15, core)
    block(7)
    make_partial(0)
    w_wait(15, 0)
    w_wait(15, 1)
    block(15)
    keys_o[...] = (acc[...] * SCALE).astype(BF16)

    @pl.when((odd == 0) & early)
    def _():
        update()

    for i in (1, 2, 3):
        g_copy(i).wait_recv()
    total = dwacc[...]
    for n in range(3):
        total = total + grecv[n].astype(F32)
    dw_o[...] = (total * SCALE).astype(BF16)

    def hand(j):
        place = (z - 2 * j - odd + NZ) % NZ
        return remote(syn_o.at[place], syn_o.at[place], ss_f.at[j], rs_f.at[j], pair)

    def taken(j):
        place = (z - 2 * j - (1 - odd) + NZ) % NZ
        return remote(syn_o.at[place], syn_o.at[place], ss_f.at[j], rs_f.at[j], pair)

    def arrive(j):
        step = 2 * j + odd
        place = (z - step + NZ) % NZ
        remote(syn_o.at[place], syn_o.at[place], ss_b.at[0], rs_b.at[step], pair).wait_recv()

    @pl.when(odd == 1)
    def _():
        arrive(0)

    hand(0).start()
    for j in (1, 7, 2, 6, 3, 5, 4):
        arrive(j)
        hand(j).start()

    @pl.when(odd == 1)
    def _():
        for n in range(2):
            remote(res.at[yl, n], res.at[yl, n], ss_q.at[n], rs_q.at[n], pair).wait_recv()

    mom_o[...] = res[yl, 0]
    glob_o[...] = res[yl, 1]
    for j in range(8):
        taken(j).wait_recv()

    for copy in sent:
        copy.wait_send()
    for j in range(1, 8):
        z_copy(j).wait_send()
    for j in range(8):
        hand(j).wait_send()

    @pl.when(odd == 1)
    def _():
        z_copy(0).wait_send()
        for copy in p_copies():
            copy.wait_send()

    @pl.when(odd == 0)
    def _():
        for d in range(1, NZ):
            syn_copy(d).wait_send()
        for copy in res_copies():
            copy.wait_send()


def write_out(*refs):
    came, go, held, sem = refs[:6], refs[6:12], refs[12:18], refs[18]
    copies = []
    for n in (1, 2, 5, 0, 3, 4):
        rows = came[n].shape[0] // 2 if n == 1 else came[n].shape[0]
        for at in range(0, came[n].shape[0], rows):
            k, part = len(copies), pl.ds(at, rows)
            copies.append((
                pltpu.make_async_copy(came[n].at[part], held[n].at[part], sem.at[0, k]),
                pltpu.make_async_copy(held[n].at[part], go[n].at[part], sem.at[1, k]),
            ))
    for copy, _ in copies:
        copy.start()
    for copy, out in copies:
        copy.wait()
        out.start()
    for _, out in copies:
        out.wait()


def on_device(tokens, local_weight, key_cot, global_weight, momentum, anchor):
    dma, vmem = pltpu.SemaphoreType.DMA, pltpu.VMEM
    scratch = [
        vmem((16, 8, 2, 16, KVW), BF16),
        vmem((TOK, 4096), BF16),
        vmem((4, 4 * TOK, ROWS), BF16),
        vmem((4 * TOK, KVW), BF16),
        vmem((TOK, KVW), F32),
        vmem((ROWS, KVW), F32),
        vmem((3, ROWS, KVW), BF16),
        vmem((3, ROWS, KVW), BF16),
        vmem((8, 16, KVW), BF16),
        vmem((8, 16, KVW), BF16),
        vmem((8, 16, KVW), BF16),
        vmem((16, 16, KVW), BF16),
        vmem((2, 3, 8, KVW), F32),
        vmem((2, 2, 8, KVW), F32),
        dma((32,)), dma((32,)),
        dma((16,)), dma((16,)),
        dma((4,)), dma((4,)),
        dma((3,)), dma((3,)),
        dma((1,)), dma((1,)),
        dma((8,)), dma((16,)),
        dma((16,)), dma((16,)),
        dma((8,)), dma((8,)),
        dma((3,)), dma((3,)),
        dma((2,)), dma((2,)),
        dma((11,)),
        pltpu.SemaphoreType.REGULAR,
    ]
    hbm, in_vmem = pl.BlockSpec(memory_space=pl.ANY), pl.BlockSpec(memory_space=vmem)
    made = pl.pallas_call(
        kernel,
        out_shape=(
            jax.ShapeDtypeStruct((TOK, KVW), BF16),
            jax.ShapeDtypeStruct((TOK, 4096), BF16),
            jax.ShapeDtypeStruct((ROWS, KVW), BF16),
            jax.ShapeDtypeStruct((8, KVW), F32),
            jax.ShapeDtypeStruct((8, KVW), F32),
            jax.ShapeDtypeStruct((16, 16, KVW), BF16),
        ),
        in_specs=[hbm] * 6,
        out_specs=[in_vmem] * 6,
        scratch_shapes=scratch,
        compiler_params=pltpu.CompilerParams(
            collective_id=0, has_side_effects=True, vmem_limit_bytes=60 * 2**20
        ),
        cost_estimate=pl.CostEstimate(
            flops=6 * 128 * 4096 * 512, bytes_accessed=4 * 2**20, transcendentals=0
        ),
        name="step",
    )(
        tokens[0],
        local_weight.reshape(8, 2, 16, KVW),
        key_cot[0],
        global_weight,
        momentum,
        anchor,
    )
    keys, gt, dw, mom, glob, syn = pl.pallas_call(
        write_out,
        out_shape=tuple(jax.ShapeDtypeStruct(m.shape, m.dtype) for m in made),
        in_specs=[hbm] * 6,
        out_specs=[hbm] * 6,
        scratch_shapes=[vmem(m.shape, m.dtype) for m in made] + [dma((2, 7))],
        compiler_params=pltpu.CompilerParams(vmem_limit_bytes=60 * 2**20),
        name="write_out",
    )(*made)
    return keys[None], gt[None], dw[None], mom, glob, syn.reshape(ROWS, KVW)


def solution(mesh):
    in_specs = (
        P("replica", "fsdp", None),
        P("replica", "fsdp", None),
        P("replica", "fsdp", None),
        P(("fsdp", "replica"), None),
        P(("fsdp", "replica"), None),
        P(("fsdp", "replica"), None),
    )
    out_specs = (
        P("replica", "fsdp", None),
        P("replica", "fsdp", None),
        P("replica", "fsdp", None),
        P(("fsdp", "replica"), None),
        P(("fsdp", "replica"), None),
        P("fsdp", None),
    )
    return jax.shard_map(
        on_device, mesh=mesh, in_specs=in_specs, out_specs=out_specs, check_vma=False
    )
```

```python
import jax
import jax.numpy as jnp
from jax import lax
from jax.experimental import pallas as pl
from jax.experimental.pallas import tpu as pltpu
from jax.sharding import PartitionSpec as P

MESH = pl.DeviceIdType.MESH
BF16, F32 = jnp.bfloat16, jnp.float32
SCALE = 1.0 / 4096**0.5
N_REPLICA = 32
NX, NZ = 4, 16
TOK, ROWS, KVW = 128, 256, 512


def kernel(
    tok, w, cot, glob, mom, anc,
    keys_o, gt_o, dw_o, mom_o, glob_o, syn_o,
    wbuf, tokv, tbuf, cbuf, acc, dwacc, gsend, grecv, sbuf, ybuf, zsum, rbuf, gma, res,
    ss_w, rs_w, ss_t, rs_t, ss_c, rs_c, ss_g, rs_g, ss_y, rs_y, ss_z, rs_z,
    ss_b, rs_b, ss_f, rs_f, ss_p, rs_p, ss_q, rs_q, loc, here,
):
    r, f = lax.axis_index("replica"), lax.axis_index("fsdp")
    z, yl = r // 2, r % 2
    x, yh, c = f // 4, (f // 2) % 2, f % 2
    xp, xm, x2 = (x + 1) % NX, (x + 3) % NX, (x + 2) % NX
    odd = (z + yl) % 2

    def at_x(other):
        return (r, other * 4 + yh * 2 + c)

    core = (r, x * 4 + yh * 2 + (1 - c))
    side = (r, x * 4 + (1 - yh) * 2 + c)
    cross = (r, x * 4 + (1 - yh) * 2 + (1 - c))
    pair = (z * 2 + (1 - yl), f)
    right, left, far = at_x(xp), at_x(xm), at_x(x2)

    def at_z(step):
        return (((z + step) % NZ) * 2 + yl, f)

    def remote(src, dst, send_sem, recv_sem, device):
        return pltpu.make_async_remote_copy(
            src_ref=src, dst_ref=dst, send_sem=send_sem, recv_sem=recv_sem,
            device_id=device, device_id_type=MESH,
        )

    def columns(xx, hh, cc):
        return pl.ds(pl.multiple_of((xx * 4 + hh * 2 + cc) * ROWS, ROWS), ROWS)

    xs_t = (x, xp, xm, x2)
    local = [
        pltpu.make_async_copy(w, wbuf.at[0], loc.at[0]),
        pltpu.make_async_copy(tok, tokv, loc.at[1]),
        pltpu.make_async_copy(cot, cbuf.at[pl.ds(0, TOK)], loc.at[2]),
        pltpu.make_async_copy(w.at[:, yl], sbuf, loc.at[3]),
        pltpu.make_async_copy(glob, gma.at[yl, 0], loc.at[4]),
        pltpu.make_async_copy(mom, gma.at[yl, 1], loc.at[5]),
        pltpu.make_async_copy(anc, gma.at[yl, 2], loc.at[6]),
    ] + [
        pltpu.make_async_copy(
            tok.at[:, columns(xs_t[i], yh, c)], tbuf.at[i, pl.ds(0, TOK)], loc.at[7 + i]
        )
        for i in range(4)
    ]
    for copy in local:
        copy.start()

    barrier = pltpu.get_barrier_semaphore()
    peers = [right, left, far, core, side, cross, pair]
    for peer in peers:
        pl.semaphore_signal(barrier, inc=1, device_id=peer, device_id_type=MESH)
    late = z >= NZ // 2

    def rank(zz):
        return jnp.where(zz < NZ // 2, zz, jnp.where(zz < 3 * NZ // 4, NZ, NZ - 1))

    mine = rank(z)
    for d in range(1, NZ):

        @pl.when(rank((z + d) % NZ) >= mine)
        def _():
            pl.semaphore_signal(barrier, inc=1, device_id=at_z(d), device_id_type=MESH)

    last = z // (NZ // 4) == 2
    above = jnp.where(late, jnp.where(last, 0, NZ // 4), NZ - 1 - z)
    below = jnp.where(late, jnp.where(last, NZ - 1, 3 * NZ // 4 - 1), z)
    pl.semaphore_wait(barrier, len(peers) + below)

    def half(ref, h):
        return ref.at[pl.ds(4 * h, 4)]

    sent = []

    def go(copy):
        copy.start()
        sent.append(copy)

    def w_send(src, slot, h, device):
        k = 2 * slot + h
        go(remote(src, half(wbuf.at[slot], h), ss_w.at[k], rs_w.at[k], device))

    def w_wait(slot, h):
        k = 2 * slot + h
        there = half(wbuf.at[slot], h)
        remote(there, there, ss_w.at[k], rs_w.at[k], core).wait_recv()

    def w_fwd(slot, h, to, device):
        w_send(half(wbuf.at[slot], h), to, h, device)

    go(remote(w.at[:, 1 - yl], ybuf, ss_y.at[0], rs_y.at[0], pair))

    def p_copies():
        return [
            remote(src, gma.at[yl, n], ss_p.at[n], rs_p.at[n], pair)
            for n, src in enumerate((glob, mom, anc))
        ]

    @pl.when(odd == 1)
    def _():
        for copy in p_copies():
            copy.start()

    w_send(half(w, 0), 1, 0, right)
    w_send(half(w, 1), 2, 1, left)
    w_send(half(w, 0), 4, 0, side)
    w_send(half(w, 0), 8, 0, core)
    w_send(half(w, 1), 8, 1, core)
    w_send(half(w, 1), 1, 1, right)
    w_send(half(w, 0), 2, 0, left)
    w_send(half(w, 1), 4, 1, side)

    def c_send(src, s, device):
        go(remote(src, cbuf.at[pl.ds(s * TOK, TOK)], ss_c.at[s], rs_c.at[s], device))

    def c_wait(s):
        there = cbuf.at[pl.ds(s * TOK, TOK)]
        remote(there, there, ss_c.at[s], rs_c.at[s], core).wait_recv()

    c_send(cot, 2, side)
    c_send(cot, 1, core)

    def t_send(i, s, hh, cc, device):
        k = 4 * i + s
        go(remote(
            tok.at[:, columns(xs_t[i], hh, cc)], tbuf.at[i, pl.ds(s * TOK, TOK)],
            ss_t.at[k], rs_t.at[k], device,
        ))

    def t_wait(i, s):
        there = tbuf.at[i, pl.ds(s * TOK, TOK)]
        remote(there, there, ss_t.at[4 * i + s], rs_t.at[4 * i + s], core).wait_recv()

    for i in (1, 2, 3, 0):
        t_send(i, 2, 1 - yh, c, side)
        t_send(i, 3, 1 - yh, 1 - c, cross)
        t_send(i, 1, yh, 1 - c, core)

    for d in range(1, NZ):

        @pl.when(rank((z + d) % NZ) < mine)
        def _():
            pl.semaphore_signal(here, inc=1, device_id=at_z(d), device_id_type=MESH)

    xs_w = (x, xm, xp, x2)

    def block(slot, first=False):
        cols = columns(
            xs_w[slot % 4],
            yh if slot % 8 < 4 else 1 - yh,
            c if slot < 8 else 1 - c,
        )
        weight = wbuf[slot].reshape(ROWS, KVW)
        part = jnp.dot(tokv[:, cols], weight, preferred_element_type=F32)
        if first:
            acc[...] = part
        else:
            acc[...] += part
        back = lax.dot_general(
            cbuf[0:TOK], weight, (((1,), (1,)), ((), ())), preferred_element_type=F32
        )
        gt_o[:, cols] = (back * SCALE).astype(BF16)

    def partial_sum(i):
        return lax.dot_general(
            tbuf[i], cbuf[...], (((0,), (0,)), ((), ())), preferred_element_type=F32
        )

    def g_copy(i):
        device = (None, right, left, far)[i]
        return remote(
            gsend.at[i - 1], grecv.at[i - 1], ss_g.at[i - 1], rs_g.at[i - 1], device
        )

    local[0].wait()
    local[1].wait()
    local[2].wait()
    block(0, first=True)
    w_wait(8, 0)
    w_wait(8, 1)
    block(8)

    local[3].wait()
    remote(ybuf, ybuf, ss_y.at[0], rs_y.at[0], pair).wait_recv()
    zsum[...] = (sbuf[...].astype(F32) + ybuf[...].astype(F32)).astype(BF16)

    def z_copy(j):
        step = 2 * j + odd
        return remote(
            zsum.at[((z + step) % NZ) // 2], rbuf.at[step], ss_z.at[j], rs_z.at[step], at_z(step)
        )

    def z_sends():
        for j in (4, 3, 5, 2, 6, 1, 7):
            z_copy(j).start()

        @pl.when(odd == 1)
        def _():
            z_copy(0).start()

    @pl.when(last)
    def _():
        z_sends()

    early = z < NZ // 4

    w_wait(1, 0)
    w_fwd(1, 0, 3, right)
    w_wait(2, 1)
    w_fwd(2, 1, 3, left)

    @pl.when(jnp.logical_not(early | last))
    def _():
        pl.semaphore_wait(here, above)
        z_sends()

    w_wait(4, 0)
    w_fwd(4, 0, 5, right)
    w_fwd(1, 0, 9, core)
    w_fwd(2, 1, 10, core)
    w_fwd(4, 0, 12, core)
    w_wait(4, 1)
    w_fwd(4, 1, 6, left)
    w_fwd(4, 1, 5, right)
    w_fwd(4, 0, 6, left)
    w_fwd(4, 1, 12, core)

    @pl.when(early)
    def _():
        pl.semaphore_wait(here, above)
        z_sends()

    w_wait(1, 1)
    w_fwd(1, 1, 9, core)
    w_wait(2, 0)
    w_fwd(2, 0, 10, core)
    block(1)
    block(2)
    block(4)
    for slot in (9, 10, 12):
        w_wait(slot, 0)
        w_wait(slot, 1)
        block(slot)
    c_wait(2)
    c_send(cbuf.at[pl.ds(2 * TOK, TOK)], 3, core)
    w_wait(3, 0)
    w_fwd(3, 0, 11, core)
    w_wait(3, 1)
    w_fwd(3, 1, 11, core)
    block(3)
    w_wait(11, 0)
    w_wait(11, 1)
    block(11)

    def make_partial(i):
        local[7 + i].wait()
        for s in (1, 2, 3):
            t_wait(i, s)
        if i == 0:
            dwacc[...] = partial_sum(0)
        else:
            gsend[i - 1] = partial_sum(i).astype(BF16)
            go(g_copy(i))

    c_wait(1)
    c_wait(3)
    make_partial(1)

    for n in (4, 5, 6):
        local[n].wait()

    def syn_copy(d):
        return remote(syn_o.at[z], syn_o.at[z], ss_b.at[d], rs_b.at[d], at_z(d))

    def res_copies():
        return [
            remote(res.at[1 - yl, n], res.at[1 - yl, n], ss_q.at[n], rs_q.at[n], pair)
            for n in range(2)
        ]

    def update():
        rbuf[0] = zsum[z // 2]
        for copy in p_copies():
            copy.wait_recv()
        for d in range(1, NZ):
            remote(rbuf.at[d], rbuf.at[d], ss_z.at[0], rs_z.at[d], pair).wait_recv()
        total = rbuf[0].astype(F32)
        for d in range(1, NZ):
            total = total + rbuf[d].astype(F32)
        fresh = []
        for owner in range(2):
            g, m, a = gma[owner, 0], gma[owner, 1], gma[owner, 2]
            pseudo = g - total[8 * owner : 8 * owner + 8] / N_REPLICA
            push = pseudo + 0.1 * (g - a)
            m_new = 0.9 * m + push
            g_new = g - 0.7 * (push + 0.9 * m_new)
            res[owner, 0] = m_new
            res[owner, 1] = g_new
            fresh.append(g_new)
        syn_o[z] = jnp.concatenate(fresh, axis=0).astype(BF16)
        for d in (8, 7, 9, 6, 10, 5, 11, 4, 12, 3, 13, 2, 14, 1, 15):
            syn_copy(d).start()
        for copy in res_copies():
            copy.start()

    @pl.when((odd == 0) & late)
    def _():
        update()

    w_wait(5, 0)
    w_fwd(5, 0, 7, right)
    w_wait(6, 1)
    w_fwd(6, 1, 7, left)
    w_fwd(5, 0, 13, core)
    w_fwd(6, 1, 14, core)
    make_partial(2)
    w_wait(5, 1)
    w_fwd(5, 1, 13, core)
    w_wait(6, 0)
    w_fwd(6, 0, 14, core)
    block(5)
    block(6)
    make_partial(3)

    @pl.when((odd == 0) & jnp.logical_not(late))
    def _():
        update()

    for slot in (13, 14):
        w_wait(slot, 0)
        w_wait(slot, 1)
        block(slot)
    w_wait(7, 0)
    w_fwd(7, 0, 15, core)
    w_wait(7, 1)
    w_fwd(7, 1, 15, core)
    block(7)
    make_partial(0)
    w_wait(15, 0)
    w_wait(15, 1)
    block(15)
    keys_o[...] = (acc[...] * SCALE).astype(BF16)

    def hand(j):
        place = (z - 2 * j - odd + NZ) % NZ
        return remote(syn_o.at[place], syn_o.at[place], ss_f.at[j], rs_f.at[j], pair)

    def taken(j):
        place = (z - 2 * j - (1 - odd) + NZ) % NZ
        return remote(syn_o.at[place], syn_o.at[place], ss_f.at[j], rs_f.at[j], pair)

    def arrive(j):
        step = 2 * j + odd
        place = (z - step + NZ) % NZ
        remote(syn_o.at[place], syn_o.at[place], ss_b.at[0], rs_b.at[step], pair).wait_recv()

    @pl.when(odd == 1)
    def _():
        arrive(0)

    hand(0).start()
    for j in (1, 7, 2, 6, 3, 5, 4):
        arrive(j)
        hand(j).start()

    for i in (1, 2, 3):
        g_copy(i).wait_recv()
    total = dwacc[...]
    for n in range(3):
        total = total + grecv[n].astype(F32)
    dw_o[...] = (total * SCALE).astype(BF16)

    @pl.when(odd == 1)
    def _():
        for n in range(2):
            remote(res.at[yl, n], res.at[yl, n], ss_q.at[n], rs_q.at[n], pair).wait_recv()

    mom_o[...] = res[yl, 0]
    glob_o[...] = res[yl, 1]
    for j in range(8):
        taken(j).wait_recv()

    for copy in sent:
        copy.wait_send()
    for j in range(1, 8):
        z_copy(j).wait_send()
    for j in range(8):
        hand(j).wait_send()

    @pl.when(odd == 1)
    def _():
        z_copy(0).wait_send()
        for copy in p_copies():
            copy.wait_send()

    @pl.when(odd == 0)
    def _():
        for d in range(1, NZ):
            syn_copy(d).wait_send()
        for copy in res_copies():
            copy.wait_send()


def write_out(*refs):
    came, go, held, sem = refs[:6], refs[6:12], refs[12:18], refs[18]
    copies = []
    for n in (1, 2, 5, 0, 3, 4):
        rows = came[n].shape[0] // 2 if n == 1 else came[n].shape[0]
        for at in range(0, came[n].shape[0], rows):
            k, part = len(copies), pl.ds(at, rows)
            copies.append((
                pltpu.make_async_copy(came[n].at[part], held[n].at[part], sem.at[0, k]),
                pltpu.make_async_copy(held[n].at[part], go[n].at[part], sem.at[1, k]),
            ))
    for copy, _ in copies:
        copy.start()
    for copy, out in copies:
        copy.wait()
        out.start()
    for _, out in copies:
        out.wait()


def on_device(tokens, local_weight, key_cot, global_weight, momentum, anchor):
    dma, vmem = pltpu.SemaphoreType.DMA, pltpu.VMEM
    scratch = [
        vmem((16, 8, 2, 16, KVW), BF16),
        vmem((TOK, 4096), BF16),
        vmem((4, 4 * TOK, ROWS), BF16),
        vmem((4 * TOK, KVW), BF16),
        vmem((TOK, KVW), F32),
        vmem((ROWS, KVW), F32),
        vmem((3, ROWS, KVW), BF16),
        vmem((3, ROWS, KVW), BF16),
        vmem((8, 16, KVW), BF16),
        vmem((8, 16, KVW), BF16),
        vmem((8, 16, KVW), BF16),
        vmem((16, 16, KVW), BF16),
        vmem((2, 3, 8, KVW), F32),
        vmem((2, 2, 8, KVW), F32),
        dma((32,)), dma((32,)),
        dma((16,)), dma((16,)),
        dma((4,)), dma((4,)),
        dma((3,)), dma((3,)),
        dma((1,)), dma((1,)),
        dma((8,)), dma((16,)),
        dma((16,)), dma((16,)),
        dma((8,)), dma((8,)),
        dma((3,)), dma((3,)),
        dma((2,)), dma((2,)),
        dma((11,)),
        pltpu.SemaphoreType.REGULAR,
    ]
    hbm, in_vmem = pl.BlockSpec(memory_space=pl.ANY), pl.BlockSpec(memory_space=vmem)
    made = pl.pallas_call(
        kernel,
        out_shape=(
            jax.ShapeDtypeStruct((TOK, KVW), BF16),
            jax.ShapeDtypeStruct((TOK, 4096), BF16),
            jax.ShapeDtypeStruct((ROWS, KVW), BF16),
            jax.ShapeDtypeStruct((8, KVW), F32),
            jax.ShapeDtypeStruct((8, KVW), F32),
            jax.ShapeDtypeStruct((16, 16, KVW), BF16),
        ),
        in_specs=[hbm] * 6,
        out_specs=[in_vmem] * 6,
        scratch_shapes=scratch,
        compiler_params=pltpu.CompilerParams(
            collective_id=0, has_side_effects=True, vmem_limit_bytes=60 * 2**20
        ),
        cost_estimate=pl.CostEstimate(
            flops=6 * 128 * 4096 * 512, bytes_accessed=4 * 2**20, transcendentals=0
        ),
        name="step",
    )(
        tokens[0],
        local_weight.reshape(8, 2, 16, KVW),
        key_cot[0],
        global_weight,
        momentum,
        anchor,
    )
    keys, gt, dw, mom, glob, syn = pl.pallas_call(
        write_out,
        out_shape=tuple(jax.ShapeDtypeStruct(m.shape, m.dtype) for m in made),
        in_specs=[hbm] * 6,
        out_specs=[hbm] * 6,
        scratch_shapes=[vmem(m.shape, m.dtype) for m in made] + [dma((2, 7))],
        compiler_params=pltpu.CompilerParams(vmem_limit_bytes=60 * 2**20),
        name="write_out",
    )(*made)
    return keys[None], gt[None], dw[None], mom, glob, syn.reshape(ROWS, KVW)


def solution(mesh):
    in_specs = (
        P("replica", "fsdp", None),
        P("replica", "fsdp", None),
        P("replica", "fsdp", None),
        P(("fsdp", "replica"), None),
        P(("fsdp", "replica"), None),
        P(("fsdp", "replica"), None),
    )
    out_specs = (
        P("replica", "fsdp", None),
        P("replica", "fsdp", None),
        P("replica", "fsdp", None),
        P(("fsdp", "replica"), None),
        P(("fsdp", "replica"), None),
        P("fsdp", None),
    )
    return jax.shard_map(
        on_device, mesh=mesh, in_specs=in_specs, out_specs=out_specs, check_vma=False
    )
```

```python
import jax
import jax.numpy as jnp
from jax import lax
from jax.experimental import pallas as pl
from jax.experimental.pallas import tpu as pltpu
from jax.sharding import PartitionSpec as P

MESH = pl.DeviceIdType.MESH
BF16, F32 = jnp.bfloat16, jnp.float32
SCALE = 1.0 / 4096**0.5
N_REPLICA = 32
NX, NZ = 4, 16
TOK, ROWS, KVW = 128, 256, 512


def kernel(
    tok, w, cot, glob, mom, anc,
    keys_h, gt_h, dw_h, mom_h, glob_h, syn_h,
    keys_o, gt_o, dw_o, mom_o, glob_o, syn_o,
    wbuf, tokv, tbuf, cbuf, acc, dwacc, gsend, grecv, sbuf, ybuf, zsum, rbuf, gma, res,
    ss_w, rs_w, ss_t, rs_t, ss_c, rs_c, ss_g, rs_g, ss_y, rs_y, ss_z, rs_z,
    ss_b, rs_b, ss_f, rs_f, ss_p, rs_p, ss_q, rs_q, loc, here, out_sem,
):
    r, f = lax.axis_index("replica"), lax.axis_index("fsdp")
    z, yl = r // 2, r % 2
    x, yh, c = f // 4, (f // 2) % 2, f % 2
    xp, xm, x2 = (x + 1) % NX, (x + 3) % NX, (x + 2) % NX
    odd = (z + yl) % 2

    def at_x(other):
        return (r, other * 4 + yh * 2 + c)

    core = (r, x * 4 + yh * 2 + (1 - c))
    side = (r, x * 4 + (1 - yh) * 2 + c)
    cross = (r, x * 4 + (1 - yh) * 2 + (1 - c))
    pair = (z * 2 + (1 - yl), f)
    right, left, far = at_x(xp), at_x(xm), at_x(x2)

    def at_z(step):
        return (((z + step) % NZ) * 2 + yl, f)

    def remote(src, dst, send_sem, recv_sem, device):
        return pltpu.make_async_remote_copy(
            src_ref=src, dst_ref=dst, send_sem=send_sem, recv_sem=recv_sem,
            device_id=device, device_id_type=MESH,
        )

    def columns(xx, hh, cc):
        return pl.ds(pl.multiple_of((xx * 4 + hh * 2 + cc) * ROWS, ROWS), ROWS)

    xs_t = (x, xp, xm, x2)
    local = [
        pltpu.make_async_copy(w, wbuf.at[0], loc.at[0]),
        pltpu.make_async_copy(tok, tokv, loc.at[1]),
        pltpu.make_async_copy(cot, cbuf.at[pl.ds(0, TOK)], loc.at[2]),
        pltpu.make_async_copy(w.at[:, yl], sbuf, loc.at[3]),
        pltpu.make_async_copy(glob, gma.at[yl, 0], loc.at[4]),
        pltpu.make_async_copy(mom, gma.at[yl, 1], loc.at[5]),
        pltpu.make_async_copy(anc, gma.at[yl, 2], loc.at[6]),
    ] + [
        pltpu.make_async_copy(
            tok.at[:, columns(xs_t[i], yh, c)], tbuf.at[i, pl.ds(0, TOK)], loc.at[7 + i]
        )
        for i in range(4)
    ]
    for copy in local:
        copy.start()

    barrier = pltpu.get_barrier_semaphore()
    peers = [right, left, far, core, side, cross, pair]
    for peer in peers:
        pl.semaphore_signal(barrier, inc=1, device_id=peer, device_id_type=MESH)
    late = z >= NZ // 2

    def rank(zz):
        return jnp.where(zz < NZ // 2, zz, jnp.where(zz < 3 * NZ // 4, NZ, NZ - 1))

    mine = rank(z)
    for d in range(1, NZ):

        @pl.when(rank((z + d) % NZ) >= mine)
        def _():
            pl.semaphore_signal(barrier, inc=1, device_id=at_z(d), device_id_type=MESH)

    last = z // (NZ // 4) == 2
    above = jnp.where(late, jnp.where(last, 0, NZ // 4), NZ - 1 - z)
    below = jnp.where(late, jnp.where(last, NZ - 1, 3 * NZ // 4 - 1), z)
    pl.semaphore_wait(barrier, len(peers) + below)
    for d in range(1, NZ):

        @pl.when(rank((z + d) % NZ) < mine)
        def _():
            pl.semaphore_signal(here, inc=1, device_id=at_z(d), device_id_type=MESH)

    def half(ref, h):
        return ref.at[pl.ds(4 * h, 4)]

    sent = []

    def go(copy):
        copy.start()
        sent.append(copy)

    def w_send(src, slot, h, device):
        k = 2 * slot + h
        go(remote(src, half(wbuf.at[slot], h), ss_w.at[k], rs_w.at[k], device))

    def w_wait(slot, h):
        k = 2 * slot + h
        there = half(wbuf.at[slot], h)
        remote(there, there, ss_w.at[k], rs_w.at[k], core).wait_recv()

    def w_fwd(slot, h, to, device):
        w_send(half(wbuf.at[slot], h), to, h, device)

    go(remote(w.at[:, 1 - yl], ybuf, ss_y.at[0], rs_y.at[0], pair))

    def p_copies():
        return [
            remote(src, gma.at[yl, n], ss_p.at[n], rs_p.at[n], pair)
            for n, src in enumerate((glob, mom, anc))
        ]

    @pl.when(odd == 1)
    def _():
        for copy in p_copies():
            copy.start()

    w_send(half(w, 0), 1, 0, right)
    w_send(half(w, 1), 2, 1, left)
    w_send(half(w, 0), 4, 0, side)
    w_send(half(w, 0), 8, 0, core)
    w_send(half(w, 1), 8, 1, core)
    w_send(half(w, 1), 1, 1, right)
    w_send(half(w, 0), 2, 0, left)
    w_send(half(w, 1), 4, 1, side)

    def c_send(src, s, device):
        go(remote(src, cbuf.at[pl.ds(s * TOK, TOK)], ss_c.at[s], rs_c.at[s], device))

    def c_wait(s):
        there = cbuf.at[pl.ds(s * TOK, TOK)]
        remote(there, there, ss_c.at[s], rs_c.at[s], core).wait_recv()

    c_send(cot, 2, side)
    c_send(cot, 1, core)

    def t_send(i, s, hh, cc, device):
        k = 4 * i + s
        go(remote(
            tok.at[:, columns(xs_t[i], hh, cc)], tbuf.at[i, pl.ds(s * TOK, TOK)],
            ss_t.at[k], rs_t.at[k], device,
        ))

    def t_wait(i, s):
        there = tbuf.at[i, pl.ds(s * TOK, TOK)]
        remote(there, there, ss_t.at[4 * i + s], rs_t.at[4 * i + s], core).wait_recv()

    for i in (1, 2, 3, 0):
        t_send(i, 2, 1 - yh, c, side)
        t_send(i, 3, 1 - yh, 1 - c, cross)
        t_send(i, 1, yh, 1 - c, core)

    xs_w = (x, xm, xp, x2)

    def block(slot, first=False):
        cols = columns(
            xs_w[slot % 4],
            yh if slot % 8 < 4 else 1 - yh,
            c if slot < 8 else 1 - c,
        )
        weight = wbuf[slot].reshape(ROWS, KVW)
        part = jnp.dot(tokv[:, cols], weight, preferred_element_type=F32)
        if first:
            acc[...] = part
        else:
            acc[...] += part
        back = lax.dot_general(
            cbuf[0:TOK], weight, (((1,), (1,)), ((), ())), preferred_element_type=F32
        )
        gt_o[:, cols] = (back * SCALE).astype(BF16)

    def partial_sum(i):
        return lax.dot_general(
            tbuf[i], cbuf[...], (((0,), (0,)), ((), ())), preferred_element_type=F32
        )

    def g_copy(i):
        device = (None, right, left, far)[i]
        return remote(
            gsend.at[i - 1], grecv.at[i - 1], ss_g.at[i - 1], rs_g.at[i - 1], device
        )

    whole = (
        (keys_o, keys_h), (gt_o, gt_h), (dw_o, dw_h), (mom_o, mom_h), (glob_o, glob_h), (syn_o, syn_h),
    )

    def result(n):
        return pltpu.make_async_copy(*whole[n], out_sem.at[n])

    local[0].wait()
    local[1].wait()
    local[2].wait()
    block(0, first=True)
    w_wait(8, 0)
    w_wait(8, 1)
    block(8)

    local[3].wait()
    remote(ybuf, ybuf, ss_y.at[0], rs_y.at[0], pair).wait_recv()
    zsum[...] = (sbuf[...].astype(F32) + ybuf[...].astype(F32)).astype(BF16)

    def z_copy(j):
        step = 2 * j + odd
        return remote(
            zsum.at[((z + step) % NZ) // 2], rbuf.at[step], ss_z.at[j], rs_z.at[step], at_z(step)
        )

    def z_sends():
        for j in (4, 3, 5, 2, 6, 1, 7):
            z_copy(j).start()

        @pl.when(odd == 1)
        def _():
            z_copy(0).start()

    @pl.when(last)
    def _():
        z_sends()

    early = z < NZ // 4

    w_wait(1, 0)
    w_fwd(1, 0, 3, right)
    w_wait(2, 1)
    w_fwd(2, 1, 3, left)

    @pl.when(jnp.logical_not(early | last))
    def _():
        pl.semaphore_wait(here, above)
        z_sends()

    w_wait(4, 0)
    w_fwd(4, 0, 5, right)
    w_fwd(1, 0, 9, core)
    w_fwd(2, 1, 10, core)
    w_fwd(4, 0, 12, core)
    w_wait(4, 1)
    w_fwd(4, 1, 6, left)
    w_fwd(4, 1, 5, right)
    w_fwd(4, 0, 6, left)
    w_fwd(4, 1, 12, core)

    @pl.when(early)
    def _():
        pl.semaphore_wait(here, above)
        z_sends()

    w_wait(1, 1)
    w_fwd(1, 1, 9, core)
    w_wait(2, 0)
    w_fwd(2, 0, 10, core)
    block(1)
    block(2)
    block(4)
    for slot in (9, 10, 12):
        w_wait(slot, 0)
        w_wait(slot, 1)
        block(slot)
    c_wait(2)
    c_send(cbuf.at[pl.ds(2 * TOK, TOK)], 3, core)
    w_wait(3, 0)
    w_fwd(3, 0, 11, core)
    w_wait(3, 1)
    w_fwd(3, 1, 11, core)
    block(3)
    w_wait(11, 0)
    w_wait(11, 1)
    block(11)

    def make_partial(i):
        local[7 + i].wait()
        for s in (1, 2, 3):
            t_wait(i, s)
        if i == 0:
            dwacc[...] = partial_sum(0)
        else:
            gsend[i - 1] = partial_sum(i).astype(BF16)
            go(g_copy(i))

    for n in (4, 5, 6):
        local[n].wait()

    def syn_copy(d):
        return remote(syn_o.at[z], syn_o.at[z], ss_b.at[d], rs_b.at[d], at_z(d))

    def res_copies():
        return [
            remote(res.at[1 - yl, n], res.at[1 - yl, n], ss_q.at[n], rs_q.at[n], pair)
            for n in range(2)
        ]

    def update():
        rbuf[0] = zsum[z // 2]
        for copy in p_copies():
            copy.wait_recv()
        for d in range(1, NZ):
            remote(rbuf.at[d], rbuf.at[d], ss_z.at[0], rs_z.at[d], pair).wait_recv()
        total = rbuf[0].astype(F32)
        for d in range(1, NZ):
            total = total + rbuf[d].astype(F32)
        fresh = []
        for owner in range(2):
            g, m, a = gma[owner, 0], gma[owner, 1], gma[owner, 2]
            pseudo = g - total[8 * owner : 8 * owner + 8] / N_REPLICA
            push = pseudo + 0.1 * (g - a)
            m_new = 0.9 * m + push
            g_new = g - 0.7 * (push + 0.9 * m_new)
            res[owner, 0] = m_new
            res[owner, 1] = g_new
            fresh.append(g_new)
        syn_o[z] = jnp.concatenate(fresh, axis=0).astype(BF16)
        for d in (8, 7, 9, 6, 10, 5, 11, 4, 12, 3, 13, 2, 14, 1, 15):
            syn_copy(d).start()
        for copy in res_copies():
            copy.start()

    @pl.when((odd == 0) & late)
    def _():
        update()

    w_wait(5, 0)
    w_fwd(5, 0, 7, right)
    w_wait(6, 1)
    w_fwd(6, 1, 7, left)
    w_fwd(5, 0, 13, core)
    w_fwd(6, 1, 14, core)
    c_wait(1)
    c_wait(3)
    make_partial(1)

    make_partial(2)
    w_wait(5, 1)
    w_fwd(5, 1, 13, core)
    w_wait(6, 0)
    w_fwd(6, 0, 14, core)
    block(5)
    block(6)
    make_partial(3)

    @pl.when((odd == 0) & jnp.logical_not(late))
    def _():
        update()

    for slot in (13, 14):
        w_wait(slot, 0)
        w_wait(slot, 1)
        block(slot)
    w_wait(7, 0)
    w_fwd(7, 0, 15, core)
    w_wait(7, 1)
    w_fwd(7, 1, 15, core)
    block(7)
    make_partial(0)
    w_wait(15, 0)
    w_wait(15, 1)
    block(15)
    keys_o[...] = (acc[...] * SCALE).astype(BF16)
    result(0).start()
    result(1).start()

    def hand(j):
        place = (z - 2 * j - odd + NZ) % NZ
        return remote(syn_o.at[place], syn_o.at[place], ss_f.at[j], rs_f.at[j], pair)

    def taken(j):
        place = (z - 2 * j - (1 - odd) + NZ) % NZ
        return remote(syn_o.at[place], syn_o.at[place], ss_f.at[j], rs_f.at[j], pair)

    def arrive(j):
        step = 2 * j + odd
        place = (z - step + NZ) % NZ
        remote(syn_o.at[place], syn_o.at[place], ss_b.at[0], rs_b.at[step], pair).wait_recv()

    @pl.when(odd == 1)
    def _():
        arrive(0)

    hand(0).start()
    for j in (1, 7, 2, 6, 3, 5, 4):
        arrive(j)
        hand(j).start()

    for i in (1, 2, 3):
        g_copy(i).wait_recv()
    total = dwacc[...]
    for n in range(3):
        total = total + grecv[n].astype(F32)
    dw_o[...] = (total * SCALE).astype(BF16)
    result(2).start()

    @pl.when(odd == 1)
    def _():
        for n in range(2):
            remote(res.at[yl, n], res.at[yl, n], ss_q.at[n], rs_q.at[n], pair).wait_recv()

    mom_o[...] = res[yl, 0]
    glob_o[...] = res[yl, 1]
    result(3).start()
    result(4).start()
    for j in range(8):
        taken(j).wait_recv()
    result(5).start()

    for n in range(6):
        result(n).wait()
    for copy in sent:
        copy.wait_send()
    for j in range(1, 8):
        z_copy(j).wait_send()
    for j in range(8):
        hand(j).wait_send()

    @pl.when(odd == 1)
    def _():
        z_copy(0).wait_send()
        for copy in p_copies():
            copy.wait_send()

    @pl.when(odd == 0)
    def _():
        for d in range(1, NZ):
            syn_copy(d).wait_send()
        for copy in res_copies():
            copy.wait_send()


def write_out(*refs):
    came, go, held, sem = refs[:6], refs[6:12], refs[12:18], refs[18]
    copies = []
    for n in (1, 2, 5, 0, 3, 4):
        rows = came[n].shape[0] // 2 if n == 1 else came[n].shape[0]
        for at in range(0, came[n].shape[0], rows):
            k, part = len(copies), pl.ds(at, rows)
            copies.append((
                pltpu.make_async_copy(came[n].at[part], held[n].at[part], sem.at[0, k]),
                pltpu.make_async_copy(held[n].at[part], go[n].at[part], sem.at[1, k]),
            ))
    for copy, _ in copies:
        copy.start()
    for copy, out in copies:
        copy.wait()
        out.start()
    for _, out in copies:
        out.wait()


def on_device(tokens, local_weight, key_cot, global_weight, momentum, anchor):
    dma, vmem = pltpu.SemaphoreType.DMA, pltpu.VMEM
    results = (
        jax.ShapeDtypeStruct((TOK, KVW), BF16),
        jax.ShapeDtypeStruct((TOK, 4096), BF16),
        jax.ShapeDtypeStruct((ROWS, KVW), BF16),
        jax.ShapeDtypeStruct((8, KVW), F32),
        jax.ShapeDtypeStruct((8, KVW), F32),
        jax.ShapeDtypeStruct((16, 16, KVW), BF16),
    )
    scratch = [vmem(m.shape, m.dtype) for m in results] + [
        vmem((16, 8, 2, 16, KVW), BF16),
        vmem((TOK, 4096), BF16),
        vmem((4, 4 * TOK, ROWS), BF16),
        vmem((4 * TOK, KVW), BF16),
        vmem((TOK, KVW), F32),
        vmem((ROWS, KVW), F32),
        vmem((3, ROWS, KVW), BF16),
        vmem((3, ROWS, KVW), BF16),
        vmem((8, 16, KVW), BF16),
        vmem((8, 16, KVW), BF16),
        vmem((8, 16, KVW), BF16),
        vmem((16, 16, KVW), BF16),
        vmem((2, 3, 8, KVW), F32),
        vmem((2, 2, 8, KVW), F32),
        dma((32,)), dma((32,)),
        dma((16,)), dma((16,)),
        dma((4,)), dma((4,)),
        dma((3,)), dma((3,)),
        dma((1,)), dma((1,)),
        dma((8,)), dma((16,)),
        dma((16,)), dma((16,)),
        dma((8,)), dma((8,)),
        dma((3,)), dma((3,)),
        dma((2,)), dma((2,)),
        dma((11,)),
        pltpu.SemaphoreType.REGULAR,
        dma((6,)),
    ]
    hbm = pl.BlockSpec(memory_space=pl.ANY)
    made = pl.pallas_call(
        kernel,
        out_shape=results,
        in_specs=[hbm] * 6,
        out_specs=[hbm] * 6,
        scratch_shapes=scratch,
        compiler_params=pltpu.CompilerParams(
            collective_id=0, has_side_effects=True, vmem_limit_bytes=60 * 2**20
        ),
        cost_estimate=pl.CostEstimate(
            flops=6 * 128 * 4096 * 512, bytes_accessed=4 * 2**20, transcendentals=0
        ),
        name="step",
    )(
        tokens[0],
        local_weight.reshape(8, 2, 16, KVW),
        key_cot[0],
        global_weight,
        momentum,
        anchor,
    )
    keys, gt, dw, mom, glob, syn = pl.pallas_call(
        write_out,
        out_shape=tuple(jax.ShapeDtypeStruct(m.shape, m.dtype) for m in made),
        in_specs=[hbm] * 6,
        out_specs=[hbm] * 6,
        scratch_shapes=[vmem(m.shape, m.dtype) for m in made] + [dma((2, 7))],
        compiler_params=pltpu.CompilerParams(vmem_limit_bytes=60 * 2**20),
        name="write_out",
    )(*made)
    return keys[None], gt[None], dw[None], mom, glob, syn.reshape(ROWS, KVW)


def solution(mesh):
    in_specs = (
        P("replica", "fsdp", None),
        P("replica", "fsdp", None),
        P("replica", "fsdp", None),
        P(("fsdp", "replica"), None),
        P(("fsdp", "replica"), None),
        P(("fsdp", "replica"), None),
    )
    out_specs = (
        P("replica", "fsdp", None),
        P("replica", "fsdp", None),
        P("replica", "fsdp", None),
        P(("fsdp", "replica"), None),
        P(("fsdp", "replica"), None),
        P("fsdp", None),
    )
    return jax.shard_map(
        on_device, mesh=mesh, in_specs=in_specs, out_specs=out_specs, check_vma=False
    )
```

```python
import jax
import jax.numpy as jnp
from jax import lax
from jax.experimental import pallas as pl
from jax.experimental.pallas import tpu as pltpu
from jax.sharding import PartitionSpec as P

MESH = pl.DeviceIdType.MESH
BF16, F32 = jnp.bfloat16, jnp.float32
SCALE = 1.0 / 4096**0.5
N_REPLICA = 32
NX, NZ = 4, 16
TOK, ROWS, KVW = 128, 256, 512


def kernel(
    tok, w, cot, glob, mom, anc,
    keys_h, gt_h, dw_h, mom_h, glob_h, syn_h,
    keys_o, gt_o, dw_o, mom_o, glob_o, syn_o,
    wbuf, tokv, tbuf, cbuf, acc, dwacc, gsend, grecv, sbuf, ybuf, zsum, rbuf, gma, res,
    ss_w, rs_w, ss_t, rs_t, ss_c, rs_c, ss_g, rs_g, ss_y, rs_y, ss_z, rs_z,
    ss_b, rs_b, ss_f, rs_f, ss_p, rs_p, ss_q, rs_q, loc, here, out_sem,
):
    r, f = lax.axis_index("replica"), lax.axis_index("fsdp")
    z, yl = r // 2, r % 2
    x, yh, c = f // 4, (f // 2) % 2, f % 2
    xp, xm, x2 = (x + 1) % NX, (x + 3) % NX, (x + 2) % NX
    odd = (z + yl) % 2

    def at_x(other):
        return (r, other * 4 + yh * 2 + c)

    core = (r, x * 4 + yh * 2 + (1 - c))
    side = (r, x * 4 + (1 - yh) * 2 + c)
    cross = (r, x * 4 + (1 - yh) * 2 + (1 - c))
    pair = (z * 2 + (1 - yl), f)
    right, left, far = at_x(xp), at_x(xm), at_x(x2)

    def at_z(step):
        return (((z + step) % NZ) * 2 + yl, f)

    def remote(src, dst, send_sem, recv_sem, device):
        return pltpu.make_async_remote_copy(
            src_ref=src, dst_ref=dst, send_sem=send_sem, recv_sem=recv_sem,
            device_id=device, device_id_type=MESH,
        )

    def columns(xx, hh, cc):
        return pl.ds(pl.multiple_of((xx * 4 + hh * 2 + cc) * ROWS, ROWS), ROWS)

    xs_t = (x, xp, xm, x2)
    local = [
        pltpu.make_async_copy(w, wbuf.at[0], loc.at[0]),
        pltpu.make_async_copy(tok, tokv, loc.at[1]),
        pltpu.make_async_copy(cot, cbuf.at[pl.ds(0, TOK)], loc.at[2]),
        pltpu.make_async_copy(w.at[:, yl], sbuf, loc.at[3]),
        pltpu.make_async_copy(glob, gma.at[yl, 0], loc.at[4]),
        pltpu.make_async_copy(mom, gma.at[yl, 1], loc.at[5]),
        pltpu.make_async_copy(anc, gma.at[yl, 2], loc.at[6]),
    ] + [
        pltpu.make_async_copy(
            tok.at[:, columns(xs_t[i], yh, c)], tbuf.at[i, pl.ds(0, TOK)], loc.at[7 + i]
        )
        for i in range(4)
    ]
    for copy in local:
        copy.start()

    barrier = pltpu.get_barrier_semaphore()
    peers = [right, left, far, core, side, cross, pair]
    for peer in peers:
        pl.semaphore_signal(barrier, inc=1, device_id=peer, device_id_type=MESH)
    late = z >= NZ // 2

    def rank(zz):
        return jnp.where(zz < NZ // 2, zz, jnp.where(zz < 3 * NZ // 4, NZ, NZ - 1))

    mine = rank(z)
    for d in range(1, NZ):

        @pl.when(rank((z + d) % NZ) >= mine)
        def _():
            pl.semaphore_signal(barrier, inc=1, device_id=at_z(d), device_id_type=MESH)

    last = z // (NZ // 4) == 2
    above = jnp.where(late, jnp.where(last, 0, NZ // 4), NZ - 1 - z)
    below = jnp.where(late, jnp.where(last, NZ - 1, 3 * NZ // 4 - 1), z)
    pl.semaphore_wait(barrier, len(peers) + below)
    for d in range(1, NZ):

        @pl.when(rank((z + d) % NZ) < mine)
        def _():
            pl.semaphore_signal(here, inc=1, device_id=at_z(d), device_id_type=MESH)

    def half(ref, h):
        return ref.at[pl.ds(4 * h, 4)]

    sent = []

    def go(copy):
        copy.start()
        sent.append(copy)

    def w_send(src, slot, h, device):
        k = 2 * slot + h
        go(remote(src, half(wbuf.at[slot], h), ss_w.at[k], rs_w.at[k], device))

    def w_wait(slot, h):
        k = 2 * slot + h
        there = half(wbuf.at[slot], h)
        remote(there, there, ss_w.at[k], rs_w.at[k], core).wait_recv()

    def w_fwd(slot, h, to, device):
        w_send(half(wbuf.at[slot], h), to, h, device)

    go(remote(w.at[:, 1 - yl], ybuf, ss_y.at[0], rs_y.at[0], pair))

    def p_copies():
        return [
            remote(src, gma.at[yl, n], ss_p.at[n], rs_p.at[n], pair)
            for n, src in enumerate((glob, mom, anc))
        ]

    @pl.when(odd == 1)
    def _():
        for copy in p_copies():
            copy.start()

    w_send(half(w, 0), 1, 0, right)
    w_send(half(w, 1), 2, 1, left)
    w_send(half(w, 0), 4, 0, side)
    w_send(half(w, 0), 8, 0, core)
    w_send(half(w, 1), 8, 1, core)
    w_send(half(w, 1), 1, 1, right)
    w_send(half(w, 0), 2, 0, left)
    w_send(half(w, 1), 4, 1, side)

    def c_send(src, s, device):
        go(remote(src, cbuf.at[pl.ds(s * TOK, TOK)], ss_c.at[s], rs_c.at[s], device))

    def c_wait(s):
        there = cbuf.at[pl.ds(s * TOK, TOK)]
        remote(there, there, ss_c.at[s], rs_c.at[s], core).wait_recv()

    c_send(cot, 2, side)
    c_send(cot, 1, core)

    def t_send(i, s, hh, cc, device):
        k = 4 * i + s
        go(remote(
            tok.at[:, columns(xs_t[i], hh, cc)], tbuf.at[i, pl.ds(s * TOK, TOK)],
            ss_t.at[k], rs_t.at[k], device,
        ))

    def t_wait(i, s):
        there = tbuf.at[i, pl.ds(s * TOK, TOK)]
        remote(there, there, ss_t.at[4 * i + s], rs_t.at[4 * i + s], core).wait_recv()

    for i in (1, 2, 3, 0):
        t_send(i, 2, 1 - yh, c, side)
        t_send(i, 3, 1 - yh, 1 - c, cross)
        t_send(i, 1, yh, 1 - c, core)

    xs_w = (x, xm, xp, x2)

    def block(slot, first=False):
        cols = columns(
            xs_w[slot % 4],
            yh if slot % 8 < 4 else 1 - yh,
            c if slot < 8 else 1 - c,
        )
        weight = wbuf[slot].reshape(ROWS, KVW)
        part = jnp.dot(tokv[:, cols], weight, preferred_element_type=F32)
        if first:
            acc[...] = part
        else:
            acc[...] += part
        back = lax.dot_general(
            cbuf[0:TOK], weight, (((1,), (1,)), ((), ())), preferred_element_type=F32
        )
        gt_o[:, cols] = (back * SCALE).astype(BF16)

    def partial_sum(i):
        return lax.dot_general(
            tbuf[i], cbuf[...], (((0,), (0,)), ((), ())), preferred_element_type=F32
        )

    def g_copy(i):
        device = (None, right, left, far)[i]
        return remote(
            gsend.at[i - 1], grecv.at[i - 1], ss_g.at[i - 1], rs_g.at[i - 1], device
        )

    whole = (
        (keys_o, keys_h), (gt_o, gt_h), (dw_o, dw_h), (mom_o, mom_h), (glob_o, glob_h), (syn_o, syn_h),
    )

    def result(n):
        return pltpu.make_async_copy(*whole[n], out_sem.at[n])

    local[0].wait()
    local[1].wait()
    local[2].wait()
    block(0, first=True)
    w_wait(8, 0)
    w_wait(8, 1)
    block(8)

    local[3].wait()
    remote(ybuf, ybuf, ss_y.at[0], rs_y.at[0], pair).wait_recv()
    zsum[...] = (sbuf[...].astype(F32) + ybuf[...].astype(F32)).astype(BF16)

    def z_copy(j):
        step = 2 * j + odd
        return remote(
            zsum.at[((z + step) % NZ) // 2], rbuf.at[step], ss_z.at[j], rs_z.at[step], at_z(step)
        )

    def z_sends():
        for j in (4, 3, 5, 2, 6, 1, 7):
            z_copy(j).start()

        @pl.when(odd == 1)
        def _():
            z_copy(0).start()

    @pl.when(last)
    def _():
        z_sends()

    early = z < NZ // 4

    w_wait(1, 0)
    w_fwd(1, 0, 3, right)
    w_wait(2, 1)
    w_fwd(2, 1, 3, left)

    @pl.when(jnp.logical_not(early | last))
    def _():
        pl.semaphore_wait(here, above)
        z_sends()

    w_wait(4, 0)
    w_fwd(4, 0, 5, right)
    w_fwd(1, 0, 9, core)
    w_fwd(2, 1, 10, core)
    w_fwd(4, 0, 12, core)
    w_wait(4, 1)
    w_fwd(4, 1, 6, left)
    w_fwd(4, 1, 5, right)
    w_fwd(4, 0, 6, left)
    w_fwd(4, 1, 12, core)

    @pl.when(early)
    def _():
        pl.semaphore_wait(here, above)
        z_sends()

    w_wait(1, 1)
    w_fwd(1, 1, 9, core)
    w_wait(2, 0)
    w_fwd(2, 0, 10, core)
    block(1)
    block(2)
    block(4)
    for slot in (9, 10, 12):
        w_wait(slot, 0)
        w_wait(slot, 1)
        block(slot)
    c_wait(2)
    c_send(cbuf.at[pl.ds(2 * TOK, TOK)], 3, core)
    w_wait(3, 0)
    w_fwd(3, 0, 11, core)
    w_wait(3, 1)
    w_fwd(3, 1, 11, core)
    block(3)
    w_wait(11, 0)
    w_wait(11, 1)
    block(11)

    def make_partial(i):
        local[7 + i].wait()
        for s in (1, 2, 3):
            t_wait(i, s)
        if i == 0:
            dwacc[...] = partial_sum(0)
        else:
            gsend[i - 1] = partial_sum(i).astype(BF16)
            go(g_copy(i))

    for n in (4, 5, 6):
        local[n].wait()

    def syn_copy(d):
        return remote(syn_o.at[z], syn_o.at[z], ss_b.at[d], rs_b.at[d], at_z(d))

    def res_copies():
        return [
            remote(res.at[1 - yl, n], res.at[1 - yl, n], ss_q.at[n], rs_q.at[n], pair)
            for n in range(2)
        ]

    def update():
        rbuf[0] = zsum[z // 2]
        for copy in p_copies():
            copy.wait_recv()
        for d in range(1, NZ):
            remote(rbuf.at[d], rbuf.at[d], ss_z.at[0], rs_z.at[d], pair).wait_recv()
        total = rbuf[0].astype(F32)
        for d in range(1, NZ):
            total = total + rbuf[d].astype(F32)
        fresh = []
        for owner in range(2):
            g, m, a = gma[owner, 0], gma[owner, 1], gma[owner, 2]
            pseudo = g - total[8 * owner : 8 * owner + 8] / N_REPLICA
            push = pseudo + 0.1 * (g - a)
            m_new = 0.9 * m + push
            g_new = g - 0.7 * (push + 0.9 * m_new)
            res[owner, 0] = m_new
            res[owner, 1] = g_new
            fresh.append(g_new)
        syn_o[z] = jnp.concatenate(fresh, axis=0).astype(BF16)
        for d in (8, 7, 9, 6, 10, 5, 11, 4, 12, 3, 13, 2, 14, 1, 15):
            syn_copy(d).start()
        for copy in res_copies():
            copy.start()

    @pl.when((odd == 0) & late)
    def _():
        update()

    w_wait(5, 0)
    w_fwd(5, 0, 7, right)
    w_wait(6, 1)
    w_fwd(6, 1, 7, left)
    w_fwd(5, 0, 13, core)
    w_fwd(6, 1, 14, core)
    c_wait(1)
    c_wait(3)
    make_partial(1)

    @pl.when((odd == 0) & jnp.logical_not(late))
    def _():
        update()

    make_partial(2)
    w_wait(5, 1)
    w_fwd(5, 1, 13, core)
    w_wait(6, 0)
    w_fwd(6, 0, 14, core)
    block(5)
    block(6)
    make_partial(3)

    for slot in (13, 14):
        w_wait(slot, 0)
        w_wait(slot, 1)
        block(slot)
    w_wait(7, 0)
    w_fwd(7, 0, 15, core)
    w_wait(7, 1)
    w_fwd(7, 1, 15, core)
    block(7)
    make_partial(0)
    w_wait(15, 0)
    w_wait(15, 1)
    block(15)
    keys_o[...] = (acc[...] * SCALE).astype(BF16)
    result(0).start()
    result(1).start()

    def hand(j):
        place = (z - 2 * j - odd + NZ) % NZ
        return remote(syn_o.at[place], syn_o.at[place], ss_f.at[j], rs_f.at[j], pair)

    def taken(j):
        place = (z - 2 * j - (1 - odd) + NZ) % NZ
        return remote(syn_o.at[place], syn_o.at[place], ss_f.at[j], rs_f.at[j], pair)

    def arrive(j):
        step = 2 * j + odd
        place = (z - step + NZ) % NZ
        remote(syn_o.at[place], syn_o.at[place], ss_b.at[0], rs_b.at[step], pair).wait_recv()

    @pl.when(odd == 1)
    def _():
        arrive(0)

    hand(0).start()
    for j in (1, 7, 2, 6, 3, 5, 4):
        arrive(j)
        hand(j).start()

    for i in (1, 2, 3):
        g_copy(i).wait_recv()
    total = dwacc[...]
    for n in range(3):
        total = total + grecv[n].astype(F32)
    dw_o[...] = (total * SCALE).astype(BF16)
    result(2).start()

    @pl.when(odd == 1)
    def _():
        for n in range(2):
            remote(res.at[yl, n], res.at[yl, n], ss_q.at[n], rs_q.at[n], pair).wait_recv()

    mom_o[...] = res[yl, 0]
    glob_o[...] = res[yl, 1]
    result(3).start()
    result(4).start()
    for j in range(8):
        taken(j).wait_recv()
    result(5).start()

    for n in range(6):
        result(n).wait()
    for copy in sent:
        copy.wait_send()
    for j in range(1, 8):
        z_copy(j).wait_send()
    for j in range(8):
        hand(j).wait_send()

    @pl.when(odd == 1)
    def _():
        z_copy(0).wait_send()
        for copy in p_copies():
            copy.wait_send()

    @pl.when(odd == 0)
    def _():
        for d in range(1, NZ):
            syn_copy(d).wait_send()
        for copy in res_copies():
            copy.wait_send()


def write_out(*refs):
    came, go, held, sem = refs[:6], refs[6:12], refs[12:18], refs[18]
    copies = []
    for n in (1, 2, 5, 0, 3, 4):
        rows = came[n].shape[0] // 2 if n == 1 else came[n].shape[0]
        for at in range(0, came[n].shape[0], rows):
            k, part = len(copies), pl.ds(at, rows)
            copies.append((
                pltpu.make_async_copy(came[n].at[part], held[n].at[part], sem.at[0, k]),
                pltpu.make_async_copy(held[n].at[part], go[n].at[part], sem.at[1, k]),
            ))
    for copy, _ in copies:
        copy.start()
    for copy, out in copies:
        copy.wait()
        out.start()
    for _, out in copies:
        out.wait()


def on_device(tokens, local_weight, key_cot, global_weight, momentum, anchor):
    dma, vmem = pltpu.SemaphoreType.DMA, pltpu.VMEM
    results = (
        jax.ShapeDtypeStruct((TOK, KVW), BF16),
        jax.ShapeDtypeStruct((TOK, 4096), BF16),
        jax.ShapeDtypeStruct((ROWS, KVW), BF16),
        jax.ShapeDtypeStruct((8, KVW), F32),
        jax.ShapeDtypeStruct((8, KVW), F32),
        jax.ShapeDtypeStruct((16, 16, KVW), BF16),
    )
    scratch = [vmem(m.shape, m.dtype) for m in results] + [
        vmem((16, 8, 2, 16, KVW), BF16),
        vmem((TOK, 4096), BF16),
        vmem((4, 4 * TOK, ROWS), BF16),
        vmem((4 * TOK, KVW), BF16),
        vmem((TOK, KVW), F32),
        vmem((ROWS, KVW), F32),
        vmem((3, ROWS, KVW), BF16),
        vmem((3, ROWS, KVW), BF16),
        vmem((8, 16, KVW), BF16),
        vmem((8, 16, KVW), BF16),
        vmem((8, 16, KVW), BF16),
        vmem((16, 16, KVW), BF16),
        vmem((2, 3, 8, KVW), F32),
        vmem((2, 2, 8, KVW), F32),
        dma((32,)), dma((32,)),
        dma((16,)), dma((16,)),
        dma((4,)), dma((4,)),
        dma((3,)), dma((3,)),
        dma((1,)), dma((1,)),
        dma((8,)), dma((16,)),
        dma((16,)), dma((16,)),
        dma((8,)), dma((8,)),
        dma((3,)), dma((3,)),
        dma((2,)), dma((2,)),
        dma((11,)),
        pltpu.SemaphoreType.REGULAR,
        dma((6,)),
    ]
    hbm = pl.BlockSpec(memory_space=pl.ANY)
    made = pl.pallas_call(
        kernel,
        out_shape=results,
        in_specs=[hbm] * 6,
        out_specs=[hbm] * 6,
        scratch_shapes=scratch,
        compiler_params=pltpu.CompilerParams(
            collective_id=0, has_side_effects=True, vmem_limit_bytes=60 * 2**20
        ),
        cost_estimate=pl.CostEstimate(
            flops=6 * 128 * 4096 * 512, bytes_accessed=4 * 2**20, transcendentals=0
        ),
        name="step",
    )(
        tokens[0],
        local_weight.reshape(8, 2, 16, KVW),
        key_cot[0],
        global_weight,
        momentum,
        anchor,
    )
    keys, gt, dw, mom, glob, syn = pl.pallas_call(
        write_out,
        out_shape=tuple(jax.ShapeDtypeStruct(m.shape, m.dtype) for m in made),
        in_specs=[hbm] * 6,
        out_specs=[hbm] * 6,
        scratch_shapes=[vmem(m.shape, m.dtype) for m in made] + [dma((2, 7))],
        compiler_params=pltpu.CompilerParams(vmem_limit_bytes=60 * 2**20),
        name="write_out",
    )(*made)
    return keys[None], gt[None], dw[None], mom, glob, syn.reshape(ROWS, KVW)


def solution(mesh):
    in_specs = (
        P("replica", "fsdp", None),
        P("replica", "fsdp", None),
        P("replica", "fsdp", None),
        P(("fsdp", "replica"), None),
        P(("fsdp", "replica"), None),
        P(("fsdp", "replica"), None),
    )
    out_specs = (
        P("replica", "fsdp", None),
        P("replica", "fsdp", None),
        P("replica", "fsdp", None),
        P(("fsdp", "replica"), None),
        P(("fsdp", "replica"), None),
        P("fsdp", None),
    )
    return jax.shard_map(
        on_device, mesh=mesh, in_specs=in_specs, out_specs=out_specs, check_vma=False
    )
```
